32 devices in a mesh: parts: 2 (over y), tok: 8 (over z, x), layer: 2 (over core).
Axes of the slice: x: 2, y: 2, z: 4, core: 2. Of those that a mesh axis runs over, the one named last changes fastest.
Arguments:
- hidden_in: bfloat16 [2, 2560, 11008], P('layer', ('parts', 'tok')), parts along dimension 1, may hold values from -6 to 6
- grad_out: bfloat16 [2, 2560, 4096], P('layer', ('parts', 'tok')), parts along dimension 1, may hold values from -6 to 6
- layer_ids: int32 [32], replicated, may hold values from 0 to 31, each once
- factor_in: bfloat16 [32, 11008, 128], P(None, 'tok'), may hold values from -0.0546875 to 0.0546875
- factor_out: bfloat16 [32, 4096, 128], P(None, 'tok'), may hold values from -0.09375 to 0.09375
Outputs:
- influence: float32 [2560, 32], P(('parts', 'tok', 'layer')), parts along dimension 0
The draws below stay inside these ranges and needn't reach their ends.
There are 2 independent parts, one for each index of `parts`. The reference program is written for one: setup_inputs(seed, part) draws one part's arguments, and reference() takes and returns one part's arrays. A program takes and returns all parts, laid end to end along the dimension named above; an argument that names none is the same for every part. Nothing has to cross between parts.
Inputs may be any that keep to these rules, and one draw needn't show every extreme that they name: `layer_ids`: each of the 32 model layers appears exactly once.
All inputs are finite; a program needn't handle non-finite values.
Results may differ from the reference program's by a relative error of at most 0.0003.
Values may be sent and summed in bfloat16 or wider, within the bound.
No kernel may reach another device: no remote copies, remote signals or barrier semaphores. Data moves between devices by JAX's collectives and lax.ppermute only.
A program may use at most 64 MiB of HBM per device.

```python
import jax
import jax.numpy as jnp
from jax import lax

D = 4096
FF = 11008
MODEL_LAYERS = 32
QUERIES = 32
RANK = 4
LAYERS = 2
TOKENS = 1280


def block_scale(own_key, extent, split, smallest, largest):
    loudness, own = 1.0, jax.random.fold_in(own_key, 6)
    for axis_at, parts in split:
        heights = jnp.exp(jax.random.uniform(jax.random.fold_in(own, axis_at), (parts,), jnp.float32, smallest / len(split), largest / len(split)))
        loudness = loudness * jnp.repeat(heights, extent[axis_at] // parts).reshape([-1 if axis == axis_at else 1 for axis in range(len(extent))])
    return loudness


def centred(key, extent, deviation, reach, cuts=(), held_as=jnp.bfloat16):
    drawn = jax.random.normal(key, extent, jnp.float32) * deviation
    if len(cuts) > 0:
        drawn = block_scale(key, extent, cuts, -0.22, 0.18) * drawn
    return jnp.clip(drawn, min=-reach, max=reach).astype(held_as)


def setup_inputs(seed: int = 0, part: int = 0) -> dict:
    keys = jax.random.split(jax.random.key(seed), 6)
    part_keys = jax.random.split(jax.random.fold_in(keys[5], part), 6)
    hidden_in = centred(part_keys[0], (LAYERS, TOKENS, FF), 1.0, 6.0, ((0, 2), (1, 8)))
    grad_out = centred(part_keys[1], (LAYERS, TOKENS, D), 1.0, 6.0, ((0, 2), (1, 8)))
    layer_ids = jax.random.permutation(keys[2], MODEL_LAYERS).astype(jnp.int32)
    factor_in = centred(keys[3], (MODEL_LAYERS, FF, QUERIES * RANK), FF ** -0.5, 0.0546875, ((1, 8),))
    factor_out = centred(keys[4], (MODEL_LAYERS, D, QUERIES * RANK), D ** -0.5, 0.09375, ((1, 8),))
    return dict(hidden_in=hidden_in, grad_out=grad_out, layer_ids=layer_ids, factor_in=factor_in, factor_out=factor_out)


def slot_scores(hidden_rows, grad_rows, inward, outward):
    in_proj = jnp.dot(hidden_rows, inward, preferred_element_type=jnp.float32)
    out_proj = jnp.dot(grad_rows, outward, preferred_element_type=jnp.float32)
    joined = in_proj * out_proj
    return joined.reshape(joined.shape[0], QUERIES, RANK).sum(axis=2)


def reference(hidden_in, grad_out, layer_ids, factor_in, factor_out):
    totals = jnp.zeros((hidden_in.shape[1], QUERIES), jnp.float32)
    for slot in range(LAYERS):
        chosen = layer_ids[slot].astype(jnp.int32)
        inward = lax.dynamic_index_in_dim(factor_in, chosen, 0, keepdims=False)
        outward = lax.dynamic_index_in_dim(factor_out, chosen, 0, keepdims=False)
        totals = totals + slot_scores(hidden_in[slot], grad_out[slot], inward, outward)
    return totals
```

```python
import functools

import jax
import jax.numpy as jnp
from jax import lax
from jax.experimental import pallas as pl
from jax.experimental.pallas import tpu as pltpu
from jax.sharding import PartitionSpec as P

QUERIES = 32
RANK = 4
AXES = ("parts", "tok", "layer")
LANES = 128


def gathered_form(hidden_in, grad_out, layer_ids, factor_in, factor_out):
    slot_index = lax.axis_index("layer") * hidden_in.shape[0]
    chosen = lax.dynamic_index_in_dim(layer_ids, slot_index, 0, keepdims=False)
    my_inward = lax.dynamic_index_in_dim(factor_in, chosen, 0, keepdims=False)
    my_outward = lax.dynamic_index_in_dim(factor_out, chosen, 0, keepdims=False)
    hidden_rows = hidden_in[0]
    grad_rows = grad_out[0]
    row_count = hidden_rows.shape[0]
    full_inward, full_outward = (
        lax.all_gather(my_inward, "tok", axis=0, tiled=True),
        lax.all_gather(my_outward, "tok", axis=0, tiled=True),
    )
    in_proj = jnp.dot(hidden_rows, full_inward, preferred_element_type=jnp.float32)
    out_proj = jnp.dot(grad_rows, full_outward, preferred_element_type=jnp.float32)
    joined = in_proj * out_proj
    scores = joined.reshape(row_count, QUERIES, RANK).sum(axis=2)
    summed = lax.psum(scores, "layer")
    halves = row_count // lax.axis_size("layer")
    return lax.dynamic_slice_in_dim(summed, lax.axis_index("layer") * halves, halves, 0)


def take_halves(half, ids_ref, in_ref, out_ref, own_ref, other_ref, sems):
    chosen = ids_ref[lax.axis_index("layer")]
    part = lax.axis_index("parts")
    tail = in_ref.shape[1] - half

    def run(first_ref, second_ref):
        copies = (
            pltpu.make_async_copy(in_ref.at[chosen, pl.ds(0, half)], first_ref, sems.at[0]),
            pltpu.make_async_copy(in_ref.at[chosen, pl.ds(half, tail)], second_ref.at[pl.ds(0, tail)], sems.at[1]),
            pltpu.make_async_copy(out_ref.at[chosen], second_ref.at[pl.ds(tail, half - tail)], sems.at[2]),
        )
        for copy in copies:
            copy.start()
        for copy in copies:
            copy.wait()

    pl.when(part == 0)(lambda: run(own_ref, other_ref))
    pl.when(part == 1)(lambda: run(other_ref, own_ref))


def add_blocks(offsets, in_rows, half, hidden_ref, grad_ref, pieces, window, acc_in, acc_out):
    part = lax.axis_index("parts")
    tok = lax.axis_index("tok")
    span = window.shape[1]
    tail = in_rows - half
    out_rows = half - tail
    for i, offset in enumerate(offsets):
        own_ref, other_ref = pieces[2 * i], pieces[2 * i + 1]
        source = tok ^ offset
        row = source * in_rows
        start = jnp.minimum(row // LANES * LANES, hidden_ref.shape[1] - span)
        shift = pl.multiple_of(row - start, 32)
        window[i] = jnp.zeros((span, LANES), jnp.bfloat16)

        def place(first_ref, second_ref):
            window[i, pl.ds(shift, half), :] = first_ref[...]
            window[i, pl.ds(pl.multiple_of(shift + half, 16), tail), :] = second_ref[:tail, :]

        pl.when(part == 0)(lambda: place(own_ref, other_ref))
        pl.when(part == 1)(lambda: place(other_ref, own_ref))
        outward = jnp.where(part == 0, other_ref[tail:, :], own_ref[tail:, :])
        acc_in = acc_in + jnp.dot(
            hidden_ref[:, pl.ds(pl.multiple_of(start, LANES), span)], window[i], preferred_element_type=jnp.float32
        )
        acc_out = acc_out + jnp.dot(
            grad_ref[:, pl.ds(pl.multiple_of(source * out_rows, LANES), out_rows)], outward,
            preferred_element_type=jnp.float32,
        )
    return acc_in, acc_out


def early(offsets, in_rows, half, hidden_ref, grad_ref, *refs):
    pieces, (in_ref, out_ref, window) = refs[:-3], refs[-3:]
    zero = jnp.zeros(in_ref.shape, jnp.float32)
    in_ref[...], out_ref[...] = add_blocks(
        offsets, in_rows, half, hidden_ref, grad_ref, pieces, window, zero, zero
    )


def late(offsets, in_rows, half, hidden_ref, grad_ref, in_ref, out_ref, *refs):
    pieces, (kept_ref, sent_ref, window) = refs[:-3], refs[-3:]
    in_proj, out_proj = add_blocks(
        offsets, in_rows, half, hidden_ref, grad_ref, pieces, window, in_ref[...], out_ref[...]
    )
    joined = in_proj * out_proj
    lane = lax.broadcasted_iota(jnp.int32, (QUERIES, LANES), 1)
    query = lax.broadcasted_iota(jnp.int32, (QUERIES, LANES), 0)
    groups = (lane // RANK == query).astype(jnp.float32)
    scores = [
        lax.dot_general(
            groups, rows, (((1,), (1,)), ((), ())), precision=lax.Precision.HIGHEST,
            preferred_element_type=jnp.float32,
        )
        for rows in jnp.split(joined, 2, axis=0)
    ]
    first = lax.axis_index("layer") == 0
    kept_ref[...] = jnp.where(first, scores[0], scores[1])
    sent_ref[...] = jnp.where(first, scores[1], scores[0])


def swapped_form(x_size, hidden_in, grad_out, layer_ids, factor_in, factor_out):
    parts, toks, layers = (lax.axis_size(a) for a in AXES)
    in_rows, out_rows = factor_in.shape[1], factor_out.shape[1]
    half = (in_rows + out_rows) // 2
    rows = hidden_in.shape[1]
    hidden, grad = hidden_in[0], grad_out[0]
    vmem = pl.BlockSpec(memory_space=pltpu.VMEM)

    def swap(value, part=0, tok=0, layer=0):
        def index(p, t, c):
            return (p * toks + t) * layers + c

        pairs = [
            (index(p, t, c), index(p ^ part, t ^ tok, c ^ layer))
            for p in range(parts) for t in range(toks) for c in range(layers)
        ]
        return lax.ppermute(value, AXES, pairs)

    across_x = functools.partial(swap, tok=1)
    across_y = functools.partial(swap, part=1)
    z_one = functools.partial(swap, tok=x_size)
    z_two = functools.partial(swap, tok=2 * x_size)

    piece = jax.ShapeDtypeStruct((half, LANES), jnp.bfloat16)
    own, other = pl.pallas_call(
        functools.partial(take_halves, half),
        out_shape=(piece, piece),
        in_specs=[pl.BlockSpec(memory_space=pltpu.SMEM)] + [pl.BlockSpec(memory_space=pl.ANY)] * 2,
        out_specs=[vmem] * 2,
        scratch_shapes=[pltpu.SemaphoreType.DMA((3,))],
    )(layer_ids, factor_in, factor_out)

    z1, z2, x0 = z_one(own), z_two(own), across_x(own)
    z1_other = z_one(other)
    y0 = across_y(x0)
    x1, x2, y2 = across_x(z1), across_x(z2), across_y(z2)
    z3 = z_one(z2)
    x3, y3 = across_x(z3), across_y(z3)
    y1, y2x = across_y(x1), across_y(x2)
    x3y = across_x(y3)

    def cost(blocks):
        return pl.CostEstimate(
            flops=2 * rows * LANES * (in_rows + out_rows) * blocks,
            bytes_accessed=2 * (rows + LANES) * (in_rows + out_rows) * blocks, transcendentals=0,
        )

    span = -(-(in_rows + LANES) // LANES) * LANES
    total = jax.ShapeDtypeStruct((rows, LANES), jnp.float32)

    def window(blocks):
        return pltpu.VMEM((blocks, span, LANES), jnp.bfloat16)

    near = (0, 1, x_size, 2 * x_size)
    sums = pl.pallas_call(
        functools.partial(early, near, in_rows, half),
        out_shape=(total, total),
        in_specs=[vmem] * 10,
        out_specs=[vmem] * 2,
        scratch_shapes=[window(4)],
        cost_estimate=cost(4),
        compiler_params=pltpu.CompilerParams(vmem_limit_bytes=24 << 20),
    )(hidden, grad, own, other, x0, y0, z1, z1_other, z2, y2)
    far = (x_size + 1, 2 * x_size + 1, 3 * x_size, 3 * x_size + 1)
    score = jax.ShapeDtypeStruct((QUERIES, rows // 2), jnp.float32)
    kept, sent = pl.pallas_call(
        functools.partial(late, far, in_rows, half),
        out_shape=(score, score),
        in_specs=[vmem] * 12,
        out_specs=[vmem] * 2,
        scratch_shapes=[window(4)],
        cost_estimate=cost(4),
        compiler_params=pltpu.CompilerParams(vmem_limit_bytes=24 << 20),
    )(hidden, grad, *sums, x1, y1, x2, y2x, z3, y3, x3, x3y)
    return (kept + swap(sent, layer=1)).T


def x_chips(mesh):
    places = [getattr(d, "coords", None) for d in mesh.devices[0, :, 0]]
    if any(p is None for p in places):
        return 0
    return len({p[0] for p in places})


def solution(mesh):
    in_specs = (
        P("layer", ("parts", "tok"), None),
        P("layer", ("parts", "tok"), None),
        P(),
        P(None, "tok", None),
        P(None, "tok", None),
    )
    out_specs = P(("parts", "tok", "layer"), None)
    x_size = x_chips(mesh)
    small = tuple(mesh.shape[a] for a in AXES) == (2, 8, 2) and x_size == 2
    form = functools.partial(swapped_form, x_size) if small else gathered_form
    return jax.shard_map(
        form, mesh=mesh, in_specs=in_specs, out_specs=out_specs, check_vma=False
    )
```

```python
import functools

import jax
import jax.numpy as jnp
from jax import lax
from jax.experimental import pallas as pl
from jax.experimental.pallas import tpu as pltpu
from jax.sharding import PartitionSpec as P

QUERIES = 32
RANK = 4
AXES = ("parts", "tok", "layer")
LANES = 128


def gathered_form(hidden_in, grad_out, layer_ids, factor_in, factor_out):
    slot_index = lax.axis_index("layer") * hidden_in.shape[0]
    chosen = lax.dynamic_index_in_dim(layer_ids, slot_index, 0, keepdims=False)
    my_inward = lax.dynamic_index_in_dim(factor_in, chosen, 0, keepdims=False)
    my_outward = lax.dynamic_index_in_dim(factor_out, chosen, 0, keepdims=False)
    hidden_rows = hidden_in[0]
    grad_rows = grad_out[0]
    row_count = hidden_rows.shape[0]
    full_inward, full_outward = (
        lax.all_gather(my_inward, "tok", axis=0, tiled=True),
        lax.all_gather(my_outward, "tok", axis=0, tiled=True),
    )
    in_proj = jnp.dot(hidden_rows, full_inward, preferred_element_type=jnp.float32)
    out_proj = jnp.dot(grad_rows, full_outward, preferred_element_type=jnp.float32)
    joined = in_proj * out_proj
    scores = joined.reshape(row_count, QUERIES, RANK).sum(axis=2)
    summed = lax.psum(scores, "layer")
    halves = row_count // lax.axis_size("layer")
    return lax.dynamic_slice_in_dim(summed, lax.axis_index("layer") * halves, halves, 0)


MOVES = (
    ((1, 0, 1), (0, 0, 1), 1, ()),
    ((0, 1, 1), (0, 0, 1), "x", ()),
    ((2, 0, 0), (0, 0, 0), 2, ()),
    ((0, 1, 0), (0, 0, 0), "x", ()),
    ((1, 1, 1), (1, 0, 1), "x", ()),
    ((3, 0, 1), (1, 0, 1), 2, ()),
    ((1, 0, 0), (1, 0, 1), "y", ((0, 1, 1),)),
    ((2, 1, 0), (2, 0, 0), "x", ((1, 0, 1), (0, 1, 1),)),
    ((3, 0, 0), (2, 0, 0), 1, ((1, 0, 1), (0, 1, 1), (0, 1, 0),)),
    ((1, 1, 0), (1, 0, 0), "x", ((1, 0, 1), (0, 1, 1), (2, 0, 0), (0, 1, 0),)),
    ((2, 0, 1), (2, 0, 0), "y", ((1, 0, 1), (0, 1, 1), (0, 1, 0), (1, 0, 0), (1, 1, 1),)),
    ((3, 1, 0), (2, 1, 0), 1, ((1, 0, 1), (0, 1, 1), (2, 0, 0), (0, 1, 0), (1, 0, 0), (1, 1, 1),)),
    ((2, 1, 1), (2, 1, 0), "y", ((1, 0, 1), (0, 1, 1), (2, 0, 0), (0, 1, 0), (1, 0, 0), (1, 1, 1), (3, 0, 1),)),
    ((3, 1, 1), (3, 0, 1), "x", ((1, 0, 1), (0, 1, 1), (2, 0, 0), (0, 1, 0), (1, 0, 0), (1, 1, 1), (2, 1, 0), (3, 0, 0),)),
)
FIRST_SUM = ((0, 0), (0, 1), (1, 0), (3, 0))


def take_halves(half, ids_ref, in_ref, out_ref, first_ref, second_ref, ids, sems):
    fetch = pltpu.make_async_copy(ids_ref, ids, sems.at[3])
    fetch.start()
    fetch.wait()
    chosen = ids[lax.axis_index("layer")]
    part = lax.axis_index("parts")
    tail = in_ref.shape[1] - half

    def run(top_ref, bottom_ref):
        copies = (
            pltpu.make_async_copy(in_ref.at[chosen, pl.ds(0, half)], top_ref, sems.at[0]),
            pltpu.make_async_copy(in_ref.at[chosen, pl.ds(half, tail)], bottom_ref.at[pl.ds(0, tail)], sems.at[1]),
            pltpu.make_async_copy(out_ref.at[chosen], bottom_ref.at[pl.ds(tail, half - tail)], sems.at[2]),
        )
        for copy in copies:
            copy.start()
        for copy in copies:
            copy.wait()

    pl.when(part == 0)(lambda: run(first_ref, second_ref))
    pl.when(part == 1)(lambda: run(second_ref, first_ref))


def add_blocks(offsets, in_rows, half, hidden_ref, grad_ref, pieces, window, acc_in, acc_out):
    part = lax.axis_index("parts")
    tok = lax.axis_index("tok")
    span = window.shape[1]
    tail = in_rows - half
    out_rows = half - tail
    for i, offset in enumerate(offsets):
        first_ref, second_ref = pieces[2 * i], pieces[2 * i + 1]
        source = tok ^ offset
        row = source * in_rows
        start = jnp.minimum(row // LANES * LANES, hidden_ref.shape[1] - span)
        shift = pl.multiple_of(row - start, 32)
        window[i] = jnp.zeros((span, LANES), jnp.bfloat16)

        def place(top_ref, bottom_ref):
            window[i, pl.ds(shift, half), :] = top_ref[...]
            window[i, pl.ds(pl.multiple_of(shift + half, 16), tail), :] = bottom_ref[:tail, :]

        pl.when(part == 0)(lambda: place(first_ref, second_ref))
        pl.when(part == 1)(lambda: place(second_ref, first_ref))
        outward = jnp.where(part == 0, second_ref[tail:, :], first_ref[tail:, :])
        acc_in = acc_in + jnp.dot(
            hidden_ref[:, pl.ds(pl.multiple_of(start, LANES), span)], window[i], preferred_element_type=jnp.float32
        )
        acc_out = acc_out + jnp.dot(
            grad_ref[:, pl.ds(pl.multiple_of(source * out_rows, LANES), out_rows)], outward,
            preferred_element_type=jnp.float32,
        )
    return acc_in, acc_out


def early(offsets, in_rows, half, hidden_ref, grad_ref, *refs):
    pieces, (in_ref, out_ref, window) = refs[:-3], refs[-3:]
    zero = jnp.zeros(in_ref.shape, jnp.float32)
    in_ref[...], out_ref[...] = add_blocks(
        offsets, in_rows, half, hidden_ref, grad_ref, pieces, window, zero, zero
    )


def late(offsets, in_rows, half, hidden_ref, grad_ref, in_ref, out_ref, *refs):
    pieces, (kept_ref, sent_ref, window) = refs[:-3], refs[-3:]
    in_proj, out_proj = add_blocks(
        offsets, in_rows, half, hidden_ref, grad_ref, pieces, window, in_ref[...], out_ref[...]
    )
    joined = in_proj * out_proj
    lane = lax.broadcasted_iota(jnp.int32, (QUERIES, LANES), 1)
    query = lax.broadcasted_iota(jnp.int32, (QUERIES, LANES), 0)
    groups = (lane // RANK == query).astype(jnp.float32)
    scores = [
        lax.dot_general(
            groups, rows, (((1,), (1,)), ((), ())), precision=lax.Precision.HIGHEST,
            preferred_element_type=jnp.float32,
        )
        for rows in jnp.split(joined, 2, axis=0)
    ]
    first = lax.axis_index("layer") == 0
    kept_ref[...] = jnp.where(first, scores[0], scores[1])
    sent_ref[...] = jnp.where(first, scores[1], scores[0])


def swapped_form(x_size, hidden_in, grad_out, layer_ids, factor_in, factor_out):
    parts, toks, layers = (lax.axis_size(a) for a in AXES)
    in_rows, out_rows = factor_in.shape[1], factor_out.shape[1]
    half = (in_rows + out_rows) // 2
    rows = hidden_in.shape[1]
    hidden, grad = hidden_in[0], grad_out[0]
    vmem = pl.BlockSpec(memory_space=pltpu.VMEM)

    def swap(value, part=0, tok=0, layer=0):
        def index(p, t, c):
            return (p * toks + t) * layers + c

        pairs = [
            (index(p, t, c), index(p ^ part, t ^ tok, c ^ layer))
            for p in range(parts) for t in range(toks) for c in range(layers)
        ]
        return lax.ppermute(value, AXES, pairs)

    partner = {"x": dict(tok=1), "y": dict(part=1), **{z: dict(tok=z * x_size) for z in (1, 2, 3)}}
    piece = jax.ShapeDtypeStruct((half, LANES), jnp.bfloat16)
    in_hbm = [pltpu.with_memory_space_constraint(a, pltpu.HBM) for a in (layer_ids, factor_in, factor_out)]
    have = dict(zip(((0, 0, 0), (0, 0, 1)), pl.pallas_call(
        functools.partial(take_halves, half),
        out_shape=(piece, piece),
        in_specs=[pl.BlockSpec(memory_space=pl.ANY)] * 3,
        out_specs=[vmem] * 2,
        scratch_shapes=[pltpu.SMEM(layer_ids.shape, layer_ids.dtype), pltpu.SemaphoreType.DMA((4,))],
        compiler_params=pltpu.CompilerParams(vmem_limit_bytes=4 << 20),
    )(*in_hbm)))
    for arrives, passed_on, across, waits in MOVES:
        value = have[passed_on]
        if waits:
            value = lax.optimization_barrier((value, *(have[w] for w in waits)))[0]
        have[arrives] = swap(value, **partner[across])

    span = -(-(in_rows + LANES) // LANES) * LANES
    total = jax.ShapeDtypeStruct((rows, LANES), jnp.float32)
    score = jax.ShapeDtypeStruct((QUERIES, rows // layers), jnp.float32)

    def products(kernel, blocks, result, *sums):
        pieces = [have[z, x, side] for z, x in blocks for side in (0, 1)]
        return pl.pallas_call(
            functools.partial(kernel, [z * x_size + x for z, x in blocks], in_rows, half),
            out_shape=(result, result),
            in_specs=[vmem] * (2 + len(sums) + len(pieces)),
            out_specs=[vmem] * 2,
            scratch_shapes=[pltpu.VMEM((len(blocks), span, LANES), jnp.bfloat16)],
            cost_estimate=pl.CostEstimate(
                flops=2 * rows * LANES * (in_rows + out_rows) * len(blocks),
                bytes_accessed=2 * (rows + LANES) * (in_rows + out_rows) * len(blocks), transcendentals=0,
            ),
            compiler_params=pltpu.CompilerParams(vmem_limit_bytes=24 << 20),
        )(hidden, grad, *sums, *pieces)

    last = [(z, x) for z in range(4) for x in range(2) if (z, x) not in FIRST_SUM]
    sums = products(early, FIRST_SUM, total)
    kept, sent = products(late, last, score, *sums)
    return (kept + swap(sent, layer=1)).T


def x_chips(mesh):
    places = [getattr(d, "coords", None) for d in mesh.devices[0, :, 0]]
    if any(p is None for p in places):
        return 0
    return len({p[0] for p in places})


def solution(mesh):
    in_specs = (
        P("layer", ("parts", "tok"), None),
        P("layer", ("parts", "tok"), None),
        P(),
        P(None, "tok", None),
        P(None, "tok", None),
    )
    out_specs = P(("parts", "tok", "layer"), None)
    x_size = x_chips(mesh)
    small = tuple(mesh.shape[a] for a in AXES) == (2, 8, 2) and x_size == 2
    form = functools.partial(swapped_form, x_size) if small else gathered_form
    return jax.shard_map(
        form, mesh=mesh, in_specs=in_specs, out_specs=out_specs, check_vma=False
    )
```

```python
import functools

import jax
import jax.numpy as jnp
from jax import lax
from jax.experimental import pallas as pl
from jax.experimental.pallas import tpu as pltpu
from jax.sharding import PartitionSpec as P

QUERIES = 32
RANK = 4
AXES = ("parts", "tok", "layer")
LANES = 128


def gathered_form(hidden_in, grad_out, layer_ids, factor_in, factor_out):
    slot_index = lax.axis_index("layer") * hidden_in.shape[0]
    chosen = lax.dynamic_index_in_dim(layer_ids, slot_index, 0, keepdims=False)
    my_inward = lax.dynamic_index_in_dim(factor_in, chosen, 0, keepdims=False)
    my_outward = lax.dynamic_index_in_dim(factor_out, chosen, 0, keepdims=False)
    hidden_rows = hidden_in[0]
    grad_rows = grad_out[0]
    row_count = hidden_rows.shape[0]
    full_inward, full_outward = (
        lax.all_gather(my_inward, "tok", axis=0, tiled=True),
        lax.all_gather(my_outward, "tok", axis=0, tiled=True),
    )
    in_proj = jnp.dot(hidden_rows, full_inward, preferred_element_type=jnp.float32)
    out_proj = jnp.dot(grad_rows, full_outward, preferred_element_type=jnp.float32)
    joined = in_proj * out_proj
    scores = joined.reshape(row_count, QUERIES, RANK).sum(axis=2)
    summed = lax.psum(scores, "layer")
    halves = row_count // lax.axis_size("layer")
    return lax.dynamic_slice_in_dim(summed, lax.axis_index("layer") * halves, halves, 0)


MOVES = (
    ((1, 0, 1), (0, 0, 1), 1, ()),
    ((0, 1, 1), (0, 0, 1), "x", ()),
    ((0, 1, 0), (0, 0, 0), "x", ()),
    ((2, 0, 0), (0, 0, 0), 2, ()),
    ((1, 1, 1), (1, 0, 1), "x", ()),
    ((3, 0, 1), (1, 0, 1), 2, ()),
    ((1, 0, 0), (1, 0, 1), "y", ((0, 1, 1),)),
    ((2, 1, 0), (2, 0, 0), "x", ((1, 0, 1), (0, 1, 1),)),
    ((3, 0, 0), (2, 0, 0), 1, ((1, 0, 1), (0, 1, 1), (0, 1, 0),)),
    ((1, 1, 0), (1, 0, 0), "x", ((1, 0, 1), (0, 1, 1), (2, 0, 0), (0, 1, 0),)),
    ((2, 0, 1), (2, 0, 0), "y", ((1, 0, 1), (0, 1, 1), (0, 1, 0), (1, 0, 0), (1, 1, 1),)),
    ((3, 1, 0), (2, 1, 0), 1, ((1, 0, 1), (0, 1, 1), (2, 0, 0), (0, 1, 0), (1, 0, 0), (1, 1, 1),)),
    ((3, 1, 1), (3, 0, 1), "x", ((1, 0, 1), (0, 1, 1), (2, 0, 0), (0, 1, 0), (1, 0, 0), (1, 1, 1), (2, 1, 0),)),
    ((2, 1, 1), (2, 1, 0), "y", ((1, 0, 1), (0, 1, 1), (2, 0, 0), (0, 1, 0), (1, 0, 0), (1, 1, 1), (3, 0, 1), (3, 0, 0),)),
)
SUMS = (
    ((0, 0), (0, 1), (1, 0), (1, 1), (2, 0), (3, 0)),
    ((3, 1),),
    ((2, 1),),
)


def take_halves(half, ids_ref, in_ref, out_ref, first_ref, second_ref, ids, sems):
    fetch = pltpu.make_async_copy(ids_ref, ids, sems.at[3])
    fetch.start()
    fetch.wait()
    chosen = ids[lax.axis_index("layer")]
    part = lax.axis_index("parts")
    tail = in_ref.shape[1] - half

    def run(top_ref, bottom_ref):
        copies = (
            pltpu.make_async_copy(in_ref.at[chosen, pl.ds(0, half)], top_ref, sems.at[0]),
            pltpu.make_async_copy(in_ref.at[chosen, pl.ds(half, tail)], bottom_ref.at[pl.ds(0, tail)], sems.at[1]),
            pltpu.make_async_copy(out_ref.at[chosen], bottom_ref.at[pl.ds(tail, half - tail)], sems.at[2]),
        )
        for copy in copies:
            copy.start()
        for copy in copies:
            copy.wait()

    pl.when(part == 0)(lambda: run(first_ref, second_ref))
    pl.when(part == 1)(lambda: run(second_ref, first_ref))


def add_blocks(offsets, in_rows, half, hidden_ref, grad_ref, pieces, window, acc_in, acc_out):
    part = lax.axis_index("parts")
    tok = lax.axis_index("tok")
    span = window.shape[1]
    tail = in_rows - half
    out_rows = half - tail
    for i, offset in enumerate(offsets):
        first_ref, second_ref = pieces[2 * i], pieces[2 * i + 1]
        source = tok ^ offset
        row = source * in_rows
        start = jnp.minimum(row // LANES * LANES, hidden_ref.shape[1] - span)
        shift = pl.multiple_of(row - start, 32)
        window[i] = jnp.zeros((span, LANES), jnp.bfloat16)

        def place(top_ref, bottom_ref):
            window[i, pl.ds(shift, half), :] = top_ref[...]
            window[i, pl.ds(pl.multiple_of(shift + half, 16), tail), :] = bottom_ref[:tail, :]

        pl.when(part == 0)(lambda: place(first_ref, second_ref))
        pl.when(part == 1)(lambda: place(second_ref, first_ref))
        outward = jnp.where(part == 0, second_ref[tail:, :], first_ref[tail:, :])
        acc_in = acc_in + jnp.dot(
            hidden_ref[:, pl.ds(pl.multiple_of(start, LANES), span)], window[i], preferred_element_type=jnp.float32
        )
        acc_out = acc_out + jnp.dot(
            grad_ref[:, pl.ds(pl.multiple_of(source * out_rows, LANES), out_rows)], outward,
            preferred_element_type=jnp.float32,
        )
    return acc_in, acc_out


def early(offsets, in_rows, half, hidden_ref, grad_ref, *refs):
    pieces, (in_ref, out_ref, window) = refs[:-3], refs[-3:]
    zero = jnp.zeros(in_ref.shape, jnp.float32)
    in_ref[...], out_ref[...] = add_blocks(
        offsets, in_rows, half, hidden_ref, grad_ref, pieces, window, zero, zero
    )


def middle(offsets, in_rows, half, hidden_ref, grad_ref, in_before, out_before, *refs):
    pieces, (in_ref, out_ref, window) = refs[:-3], refs[-3:]
    in_ref[...], out_ref[...] = add_blocks(
        offsets, in_rows, half, hidden_ref, grad_ref, pieces, window, in_before[...], out_before[...]
    )


def late(offsets, in_rows, half, hidden_ref, grad_ref, in_ref, out_ref, *refs):
    pieces, (kept_ref, sent_ref, window) = refs[:-3], refs[-3:]
    in_proj, out_proj = add_blocks(
        offsets, in_rows, half, hidden_ref, grad_ref, pieces, window, in_ref[...], out_ref[...]
    )
    joined = in_proj * out_proj
    lane = lax.broadcasted_iota(jnp.int32, (QUERIES, LANES), 1)
    query = lax.broadcasted_iota(jnp.int32, (QUERIES, LANES), 0)
    groups = (lane // RANK == query).astype(jnp.float32)
    scores = [
        lax.dot_general(
            groups, rows, (((1,), (1,)), ((), ())), precision=lax.Precision.HIGHEST,
            preferred_element_type=jnp.float32,
        )
        for rows in jnp.split(joined, 2, axis=0)
    ]
    first = lax.axis_index("layer") == 0
    kept_ref[...] = jnp.where(first, scores[0], scores[1])
    sent_ref[...] = jnp.where(first, scores[1], scores[0])


def swapped_form(x_size, hidden_in, grad_out, layer_ids, factor_in, factor_out):
    parts, toks, layers = (lax.axis_size(a) for a in AXES)
    in_rows, out_rows = factor_in.shape[1], factor_out.shape[1]
    half = (in_rows + out_rows) // 2
    rows = hidden_in.shape[1]
    hidden, grad = hidden_in[0], grad_out[0]
    vmem = pl.BlockSpec(memory_space=pltpu.VMEM)

    def swap(value, part=0, tok=0, layer=0):
        def index(p, t, c):
            return (p * toks + t) * layers + c

        pairs = [
            (index(p, t, c), index(p ^ part, t ^ tok, c ^ layer))
            for p in range(parts) for t in range(toks) for c in range(layers)
        ]
        return lax.ppermute(value, AXES, pairs)

    partner = {"x": dict(tok=1), "y": dict(part=1), **{z: dict(tok=z * x_size) for z in (1, 2, 3)}}
    piece = jax.ShapeDtypeStruct((half, LANES), jnp.bfloat16)
    in_hbm = [pltpu.with_memory_space_constraint(a, pltpu.HBM) for a in (layer_ids, factor_in, factor_out)]
    have = dict(zip(((0, 0, 0), (0, 0, 1)), pl.pallas_call(
        functools.partial(take_halves, half),
        out_shape=(piece, piece),
        in_specs=[pl.BlockSpec(memory_space=pl.ANY)] * 3,
        out_specs=[vmem] * 2,
        scratch_shapes=[pltpu.SMEM(layer_ids.shape, layer_ids.dtype), pltpu.SemaphoreType.DMA((4,))],
        compiler_params=pltpu.CompilerParams(vmem_limit_bytes=4 << 20),
    )(*in_hbm)))
    for arrives, passed_on, across, waits in MOVES:
        value = have[passed_on]
        if waits:
            value = lax.optimization_barrier((value, *(have[w] for w in waits)))[0]
        have[arrives] = swap(value, **partner[across])

    span = -(-(in_rows + LANES) // LANES) * LANES
    total = jax.ShapeDtypeStruct((rows, LANES), jnp.float32)
    score = jax.ShapeDtypeStruct((QUERIES, rows // layers), jnp.float32)

    def products(kernel, blocks, result, *sums):
        pieces = [have[z, x, side] for z, x in blocks for side in (0, 1)]
        return pl.pallas_call(
            functools.partial(kernel, [z * x_size + x for z, x in blocks], in_rows, half),
            out_shape=(result, result),
            in_specs=[vmem] * (2 + len(sums) + len(pieces)),
            out_specs=[vmem] * 2,
            scratch_shapes=[pltpu.VMEM((len(blocks), span, LANES), jnp.bfloat16)],
            cost_estimate=pl.CostEstimate(
                flops=2 * rows * LANES * (in_rows + out_rows) * len(blocks),
                bytes_accessed=2 * (rows + LANES) * (in_rows + out_rows) * len(blocks), transcendentals=0,
            ),
            compiler_params=pltpu.CompilerParams(vmem_limit_bytes=24 << 20),
        )(hidden, grad, *sums, *pieces)

    sums = products(early, SUMS[0], total)
    for blocks in SUMS[1:-1]:
        sums = products(middle, blocks, total, *sums)
    kept, sent = products(late, SUMS[-1], score, *sums)
    return (kept + swap(sent, layer=1)).T


def x_chips(mesh):
    places = [getattr(d, "coords", None) for d in mesh.devices[0, :, 0]]
    if any(p is None for p in places):
        return 0
    return len({p[0] for p in places})


def solution(mesh):
    in_specs = (
        P("layer", ("parts", "tok"), None),
        P("layer", ("parts", "tok"), None),
        P(),
        P(None, "tok", None),
        P(None, "tok", None),
    )
    out_specs = P(("parts", "tok", "layer"), None)
    x_size = x_chips(mesh)
    small = tuple(mesh.shape[a] for a in AXES) == (2, 8, 2) and x_size == 2
    form = functools.partial(swapped_form, x_size) if small else gathered_form
    return jax.shard_map(
        form, mesh=mesh, in_specs=in_specs, out_specs=out_specs, check_vma=False
    )
```

```python
import functools

import jax
import jax.numpy as jnp
from jax import lax
from jax.experimental import pallas as pl
from jax.experimental.pallas import tpu as pltpu
from jax.sharding import PartitionSpec as P

QUERIES = 32
RANK = 4
AXES = ("parts", "tok", "layer")
LANES = 128


def gathered_form(hidden_in, grad_out, layer_ids, factor_in, factor_out):
    slot_index = lax.axis_index("layer") * hidden_in.shape[0]
    chosen = lax.dynamic_index_in_dim(layer_ids, slot_index, 0, keepdims=False)
    my_inward = lax.dynamic_index_in_dim(factor_in, chosen, 0, keepdims=False)
    my_outward = lax.dynamic_index_in_dim(factor_out, chosen, 0, keepdims=False)
    hidden_rows = hidden_in[0]
    grad_rows = grad_out[0]
    row_count = hidden_rows.shape[0]
    full_inward, full_outward = (
        lax.all_gather(my_inward, "tok", axis=0, tiled=True),
        lax.all_gather(my_outward, "tok", axis=0, tiled=True),
    )
    in_proj = jnp.dot(hidden_rows, full_inward, preferred_element_type=jnp.float32)
    out_proj = jnp.dot(grad_rows, full_outward, preferred_element_type=jnp.float32)
    joined = in_proj * out_proj
    scores = joined.reshape(row_count, QUERIES, RANK).sum(axis=2)
    summed = lax.psum(scores, "layer")
    halves = row_count // lax.axis_size("layer")
    return lax.dynamic_slice_in_dim(summed, lax.axis_index("layer") * halves, halves, 0)


MOVES = (
    ((1, 0, 1), (0, 0, 1), 1, ()),
    ((0, 1, 1), (0, 0, 1), "x", ()),
    ((0, 1, 0), (0, 0, 0), "x", ()),
    ((2, 0, 0), (0, 0, 0), 2, ()),
    ((1, 1, 1), (1, 0, 1), "x", ()),
    ((3, 0, 1), (1, 0, 1), 2, ()),
    ((1, 0, 0), (1, 0, 1), "y", ((0, 1, 1),)),
    ((3, 0, 0), (2, 0, 0), 1, ((1, 0, 1), (0, 1, 1), (0, 1, 0),)),
    ((2, 1, 0), (2, 0, 0), "x", ((1, 0, 1), (0, 1, 1),)),
    ((1, 1, 0), (1, 0, 0), "x", ((1, 0, 1), (0, 1, 1), (2, 0, 0), (0, 1, 0),)),
    ((2, 0, 1), (2, 0, 0), "y", ((1, 0, 1), (0, 1, 1), (0, 1, 0), (1, 0, 0), (1, 1, 1),)),
    ((3, 1, 0), (2, 1, 0), 1, ((1, 0, 1), (0, 1, 1), (2, 0, 0), (0, 1, 0), (1, 0, 0), (1, 1, 1),)),
    ((3, 1, 1), (3, 0, 1), "x", ((1, 0, 1), (0, 1, 1), (2, 0, 0), (0, 1, 0), (1, 0, 0), (1, 1, 1), (2, 1, 0),)),
    ((2, 1, 1), (2, 1, 0), "y", ((1, 0, 1), (0, 1, 1), (2, 0, 0), (0, 1, 0), (1, 0, 0), (1, 1, 1), (3, 0, 1), (3, 0, 0),)),
)
SUMS = (
    ((0, 0), (0, 1), (1, 0), (1, 1), (2, 0), (3, 0)),
    ((3, 1),),
    ((2, 1),),
)


def take_halves(half, ids_ref, in_ref, out_ref, first_ref, second_ref, sems):
    chosen = ids_ref[lax.axis_index("layer")]
    part = lax.axis_index("parts")
    tail = in_ref.shape[1] - half

    def run(top_ref, bottom_ref):
        copies = (
            pltpu.make_async_copy(in_ref.at[chosen, pl.ds(0, half)], top_ref, sems.at[0]),
            pltpu.make_async_copy(in_ref.at[chosen, pl.ds(half, tail)], bottom_ref.at[pl.ds(0, tail)], sems.at[1]),
            pltpu.make_async_copy(out_ref.at[chosen], bottom_ref.at[pl.ds(tail, half - tail)], sems.at[2]),
        )
        for copy in copies:
            copy.start()
        for copy in copies:
            copy.wait()

    pl.when(part == 0)(lambda: run(first_ref, second_ref))
    pl.when(part == 1)(lambda: run(second_ref, first_ref))


def add_blocks(offsets, in_rows, half, hidden_ref, grad_ref, pieces, window, acc_in, acc_out):
    part = lax.axis_index("parts")
    tok = lax.axis_index("tok")
    span = window.shape[1]
    tail = in_rows - half
    out_rows = half - tail
    for i, offset in enumerate(offsets):
        first_ref, second_ref = pieces[2 * i], pieces[2 * i + 1]
        source = tok ^ offset
        row = source * in_rows
        start = jnp.minimum(row // LANES * LANES, hidden_ref.shape[1] - span)
        shift = pl.multiple_of(row - start, 32)
        window[i] = jnp.zeros((span, LANES), jnp.bfloat16)

        def place(top_ref, bottom_ref):
            window[i, pl.ds(shift, half), :] = top_ref[...]
            window[i, pl.ds(pl.multiple_of(shift + half, 16), tail), :] = bottom_ref[:tail, :]

        pl.when(part == 0)(lambda: place(first_ref, second_ref))
        pl.when(part == 1)(lambda: place(second_ref, first_ref))
        outward = jnp.where(part == 0, second_ref[tail:, :], first_ref[tail:, :])
        acc_in = acc_in + jnp.dot(
            hidden_ref[:, pl.ds(pl.multiple_of(start, LANES), span)], window[i], preferred_element_type=jnp.float32
        )
        acc_out = acc_out + jnp.dot(
            grad_ref[:, pl.ds(pl.multiple_of(source * out_rows, LANES), out_rows)], outward,
            preferred_element_type=jnp.float32,
        )
    return acc_in, acc_out


def early(offsets, in_rows, half, hidden_ref, grad_ref, *refs):
    pieces, (in_ref, out_ref, window) = refs[:-3], refs[-3:]
    zero = jnp.zeros(in_ref.shape, jnp.float32)
    in_ref[...], out_ref[...] = add_blocks(
        offsets, in_rows, half, hidden_ref, grad_ref, pieces, window, zero, zero
    )


def middle(offsets, in_rows, half, hidden_ref, grad_ref, in_before, out_before, *refs):
    pieces, (in_ref, out_ref, window) = refs[:-3], refs[-3:]
    in_ref[...], out_ref[...] = add_blocks(
        offsets, in_rows, half, hidden_ref, grad_ref, pieces, window, in_before[...], out_before[...]
    )


def late(offsets, in_rows, half, hidden_ref, grad_ref, in_ref, out_ref, *refs):
    pieces, (kept_ref, sent_ref, window) = refs[:-3], refs[-3:]
    in_proj, out_proj = add_blocks(
        offsets, in_rows, half, hidden_ref, grad_ref, pieces, window, in_ref[...], out_ref[...]
    )
    joined = in_proj * out_proj
    lane = lax.broadcasted_iota(jnp.int32, (QUERIES, LANES), 1)
    query = lax.broadcasted_iota(jnp.int32, (QUERIES, LANES), 0)
    groups = (lane // RANK == query).astype(jnp.float32)
    scores = [
        lax.dot_general(
            groups, rows, (((1,), (1,)), ((), ())), precision=lax.Precision.HIGHEST,
            preferred_element_type=jnp.float32,
        )
        for rows in jnp.split(joined, 2, axis=0)
    ]
    first = lax.axis_index("layer") == 0
    kept_ref[...] = jnp.where(first, scores[0], scores[1])
    sent_ref[...] = jnp.where(first, scores[1], scores[0])


def swapped_form(x_size, hidden_in, grad_out, layer_ids, factor_in, factor_out):
    parts, toks, layers = (lax.axis_size(a) for a in AXES)
    in_rows, out_rows = factor_in.shape[1], factor_out.shape[1]
    half = (in_rows + out_rows) // 2
    rows = hidden_in.shape[1]
    hidden, grad = hidden_in[0], grad_out[0]
    vmem = pl.BlockSpec(memory_space=pltpu.VMEM)

    def swap(value, part=0, tok=0, layer=0):
        def index(p, t, c):
            return (p * toks + t) * layers + c

        pairs = [
            (index(p, t, c), index(p ^ part, t ^ tok, c ^ layer))
            for p in range(parts) for t in range(toks) for c in range(layers)
        ]
        return lax.ppermute(value, AXES, pairs)

    partner = {"x": dict(tok=1), "y": dict(part=1), **{z: dict(tok=z * x_size) for z in (1, 2, 3)}}
    piece = jax.ShapeDtypeStruct((half, LANES), jnp.bfloat16)
    in_hbm = [pltpu.with_memory_space_constraint(a, pltpu.HBM) for a in (layer_ids, factor_in, factor_out)]
    have = dict(zip(((0, 0, 0), (0, 0, 1)), pl.pallas_call(
        functools.partial(take_halves, half),
        out_shape=(piece, piece),
        in_specs=[pl.BlockSpec(memory_space=pltpu.SMEM)] + [pl.BlockSpec(memory_space=pl.ANY)] * 2,
        out_specs=[vmem] * 2,
        scratch_shapes=[pltpu.SemaphoreType.DMA((3,))],
        compiler_params=pltpu.CompilerParams(vmem_limit_bytes=4 << 20),
    )(*in_hbm)))
    for arrives, passed_on, across, waits in MOVES:
        value = have[passed_on]
        if waits:
            value = lax.optimization_barrier((value, *(have[w] for w in waits)))[0]
        have[arrives] = swap(value, **partner[across])

    span = -(-(in_rows + LANES) // LANES) * LANES
    total = jax.ShapeDtypeStruct((rows, LANES), jnp.float32)
    score = jax.ShapeDtypeStruct((QUERIES, rows // layers), jnp.float32)

    def products(kernel, blocks, result, *sums):
        pieces = [have[z, x, side] for z, x in blocks for side in (0, 1)]
        return pl.pallas_call(
            functools.partial(kernel, [z * x_size + x for z, x in blocks], in_rows, half),
            out_shape=(result, result),
            in_specs=[vmem] * (2 + len(sums) + len(pieces)),
            out_specs=[vmem] * 2,
            scratch_shapes=[pltpu.VMEM((len(blocks), span, LANES), jnp.bfloat16)],
            cost_estimate=pl.CostEstimate(
                flops=2 * rows * LANES * (in_rows + out_rows) * len(blocks),
                bytes_accessed=2 * (rows + LANES) * (in_rows + out_rows) * len(blocks), transcendentals=0,
            ),
            compiler_params=pltpu.CompilerParams(vmem_limit_bytes=24 << 20),
        )(hidden, grad, *sums, *pieces)

    sums = products(early, SUMS[0], total)
    for blocks in SUMS[1:-1]:
        sums = products(middle, blocks, total, *sums)
    kept, sent = products(late, SUMS[-1], score, *sums)
    return (kept + swap(sent, layer=1)).T


def x_chips(mesh):
    places = [getattr(d, "coords", None) for d in mesh.devices[0, :, 0]]
    if any(p is None for p in places):
        return 0
    return len({p[0] for p in places})


def solution(mesh):
    in_specs = (
        P("layer", ("parts", "tok"), None),
        P("layer", ("parts", "tok"), None),
        P(),
        P(None, "tok", None),
        P(None, "tok", None),
    )
    out_specs = P(("parts", "tok", "layer"), None)
    x_size = x_chips(mesh)
    small = tuple(mesh.shape[a] for a in AXES) == (2, 8, 2) and x_size == 2
    form = functools.partial(swapped_form, x_size) if small else gathered_form
    return jax.shard_map(
        form, mesh=mesh, in_specs=in_specs, out_specs=out_specs, check_vma=False
    )
```
